128 devices in a mesh: op: 8 (over y, core), tm: 16 (over z, x).
Axes of the slice: x: 4, y: 4, z: 4, core: 2. Of those that a mesh axis runs over, the one named last changes fastest.
Arguments:
- mesons: float32 [8, 32, 2, 384, 384], P('op', 'tm'), may hold values from -6 to 6
- perambulator: float32 [32, 2, 384, 384], P('tm', None, 'op'), may hold values from -0.21875 to 0.21875
- graph_list: int32 [64, 4], P('op'), may hold values from -2 to 7, as said below
Outputs:
- diagrams: float32 [384, 6144], P('op', 'tm')
The draws below stay inside these ranges and needn't reach their ends.
Inputs may be any that keep to these rules, and one draw needn't show every extreme that they name: `graph_list`: each row is a product slot of the op index that holds it: first operator id and second operator id (0 to 7, the second taken at the sink time), diagram id (0 to 7) and an integer weight. Weight 0 marks an empty slot; live weights are -2, -1, 1 or 2 and the live slots of an op index come first. In every draw some op index has all 8 slots live.
All inputs are finite; a program needn't handle non-finite values.
Results may differ from the reference program's by a relative error of at most 0.0003.
Values sent between devices are 32-bit elements; how exact they have to be, the bound alone decides.
A program may use at most 128 MiB of HBM per device.

```python
import jax
import jax.numpy as jnp
from jax import lax

N = 384
TT_DEV = 2
PSLOT = 8
DIAG = 8
OPS = 8
TIMES = 32
N_OP = 8


def draw_graph_list(key, part):
    subkeys = jax.random.split(key, 7)
    total_slots = N_OP * PSLOT
    slot_index = jnp.arange(total_slots, dtype=jnp.int32) % PSLOT
    device_index = jnp.arange(total_slots, dtype=jnp.int32) // PSLOT
    counts = jax.random.randint(subkeys[0], (N_OP,), 1, PSLOT // 2 + 1)
    busiest = jax.random.randint(subkeys[1], (), 0, N_OP)
    counts = jnp.where(jnp.arange(N_OP, dtype=jnp.int32) == busiest, PSLOT, counts)
    first_operand = jax.random.randint(subkeys[2], (total_slots,), 0, OPS)
    second_operand = jax.random.randint(subkeys[3], (total_slots,), 0, OPS)
    offsets = jax.random.randint(subkeys[4], (), 0, DIAG)
    random_diagram = jax.random.randint(subkeys[5], (total_slots,), 0, DIAG)
    diagram = jnp.where(device_index == busiest, (slot_index + offsets) % DIAG, random_diagram)
    level = jax.random.randint(subkeys[6], (total_slots,), 0, 4)
    weight = level - 2 + (level >= 2).astype(jnp.int32)
    weight = jnp.where(slot_index < counts[device_index], weight, 0)
    return jnp.stack([first_operand, second_operand, diagram, weight], axis=1).astype(jnp.int32)


def block_levels(own_key, dims, pieces, low, top_value):
    factor_of = 1.0
    for axis_at, shards_of in pieces:
        heights = jax.random.uniform(jax.random.fold_in(jax.random.fold_in(own_key, 6), axis_at), (shards_of,), jnp.float32, low / len(pieces), top_value / len(pieces))
        factor_of = factor_of * jnp.repeat(jnp.exp(heights), dims[axis_at] // shards_of).reshape((-1,) + (1,) * (len(dims) - 1 - axis_at))
    return factor_of


def centred(key, shape, spread, reach, cuts=(), held_as=jnp.bfloat16):
    drawn = spread * jax.random.normal(key, shape, jnp.float32)
    if cuts:
        drawn = drawn * block_levels(key, shape, cuts, -0.22, 0.18)
    return jnp.clip(drawn, -reach, reach).astype(held_as)


def setup_inputs(seed: int = 0) -> dict:
    splits = jax.random.split(jax.random.key(seed), 4)
    return {
        "mesons": centred(splits[0], (OPS, TIMES, 2, N, N), 1.0, 6.0, ((0, 8), (1, 16)), jnp.float32),
        "perambulator": centred(splits[1], (TIMES, 2, N, N), (2 * N) ** -0.5, 0.21875, ((0, 16), (2, 8)), jnp.float32),
        "graph_list": draw_graph_list(jax.random.fold_in(splits[3], 71), 0),
    }


HIGHEST = lax.Precision.HIGHEST


def matmul_high(first, second):
    return jnp.matmul(first, second, precision=HIGHEST)


def complex_product(first, second):
    first_real = first[..., 0, :, :]
    first_imag = first[..., 1, :, :]
    second_real = second[..., 0, :, :]
    second_imag = second[..., 1, :, :]
    real_part = matmul_high(first_real, second_real) - matmul_high(first_imag, second_imag)
    imag_part = matmul_high(first_real, second_imag) + matmul_high(first_imag, second_real)
    return jnp.stack([real_part, imag_part], axis=-3)


def adjoint(matrix):
    swapped = jnp.swapaxes(matrix, -1, -2)
    return jnp.stack([swapped[..., 0, :, :], -swapped[..., 1, :, :]], axis=-3)


def dress(mesons, tau):
    return complex_product(adjoint(tau), complex_product(mesons, tau))


def reference(mesons, perambulator, graph_list):
    times_all = mesons.shape[1]

    def dress_time(time_index):
        return dress(mesons[:, time_index], perambulator[time_index][None])

    dressed = lax.map(dress_time, jnp.arange(times_all, dtype=jnp.int32))
    factor = (2.0 * N) ** -0.5 / times_all

    def over_times(totals, time_index):
        later_index = (time_index + TT_DEV) % times_all
        current = dressed[time_index]
        sink_side = dressed[later_index]

        def over_entries(totals, entry):
            def include(totals):
                product = complex_product(current[entry[0]], sink_side[entry[1]])
                previous = totals[entry[2]]
                return totals.at[entry[2]].set(previous + (entry[3].astype(jnp.float32) * factor) * product)

            return lax.cond(entry[3] != 0, include, lambda unchanged: unchanged, totals), None

        totals, _ = lax.scan(over_entries, totals, graph_list)
        return totals, None

    totals = jnp.zeros((DIAG, 2, N, N), jnp.float32)
    totals, _ = lax.scan(over_times, totals, jnp.arange(times_all, dtype=jnp.int32))
    return jnp.transpose(totals, (2, 0, 1, 3)).reshape(N, DIAG * 2 * N)
```

```python
import functools

import jax
import jax.numpy as jnp
from jax import lax
from jax.experimental import pallas as pl
from jax.experimental.pallas import tpu as pltpu
from jax.sharding import PartitionSpec as P

N = 384
DIAG = 8
OPS = 8
BLK = N // 8
CH = 128
NCH = N // CH
HALF = CH // 2
SUB = HALF // 4
F32 = jnp.float32
BF16 = jnp.bfloat16
MESH = pl.DeviceIdType.MESH
RELS = [(dy, dc) for dy in (1, 3, 2, 0) for dc in (0, 1)]


def halves(value):
    high = value.astype(BF16)
    return high, (value - high.astype(F32)).astype(BF16)


def dot3(a_high, a_low, b_high, b_low):
    dot = functools.partial(jnp.dot, preferred_element_type=F32)
    return dot(a_high, b_high) + (dot(a_high, b_low) + dot(a_low, b_high))


def rows(index, size):
    return pl.ds(pl.multiple_of(index * size, size), size)


def kernel(
    mesons, tau, table, out,
    wall, wsum, wsm, taus, lhs1, lhs2, rhs, dres, drest, abuf, bbuf, ehi, elo,
    lmain, prod, cbuf, s1x, s1z, r0, r1, s2x, s2z, sbuf, fin,
    w_s, w_r, w_l, t_s, t_r, f_s, f_r, a_s, a_r, b_s, b_r, c_s, c_r,
    x1_s, x1_r, z1_s, z1_r, x2_s, x2_r, z2_s, z2_r, y_s, y_r,
):
    op, tm = lax.axis_index("op"), lax.axis_index("tm")
    y, c, z, x = op // 2, op % 2, tm // 4, tm % 4

    def device(dy=0, dc=0, dz=0, dx=0):
        return (((y + dy) % 4) * 2 + (c + dc) % 2, ((z + dz) % 4) * 4 + (x + dx) % 4)

    def column(dy, dc, dj):
        return (((y + dy) % 4) * 2 + (c + dc) % 2, (tm + dj + 16) % 16)

    def source(dy, dc):
        return ((y - dy + 4) % 4) * 2 + (c + dc) % 2

    def remote(src, dst, send, recv, where):
        return pltpu.make_async_remote_copy(
            src_ref=src, dst_ref=dst, send_sem=send, recv_sem=recv, device_id=where, device_id_type=MESH
        )

    greet = [column(dy, dc, dj) for dj in (0, 1, -1) for dy, dc in RELS if (dy, dc, dj) != (0, 0, 0)]
    greet += [device(dx=k) for k in (1, 2, 3)] + [device(dz=k) for k in (1, 2, 3)]
    barrier = pltpu.get_barrier_semaphore()
    for where in greet:
        pl.semaphore_signal(barrier, inc=1, device_id=where, device_id_type=MESH)
    pl.semaphore_wait(barrier, len(greet))

    waits = []

    near = [(k, dy, dc) for k, (dy, dc) in enumerate(RELS) if (dy, dc) != (0, 0)]

    def tau_copy(t, dy):
        dc = 1 if dy == 0 else 0
        return remote(
            tau.at[t], taus.at[t, :, rows(op, BLK), :], t_s.at[t, dy], t_r.at[t, dy], device(dy=dy, dc=dc)
        )

    def tau_forward(t, dy):
        block = taus.at[t, :, rows(source(dy, 0), BLK), :]
        return remote(block, block, f_s.at[t, dy], f_r.at[t, dy], device(dc=1))

    def table_copy(k, dy, dc):
        return remote(table, wall.at[op], w_s.at[k], w_r.at[k], device(dy=dy, dc=dc))

    for dy in (1, 3, 2, 0):
        tau_copy(0, dy).start()
    for dy in (1, 3, 2, 0):
        tau_copy(1, dy).start()
    for k, dy, dc in near:
        table_copy(k, dy, dc).start()
    wall[op] = table[...]
    for t in range(2):
        taus[t, :, rows(op, BLK), :] = tau[t]
        for p in range(2):
            high, low = halves(mesons[0, t, p])
            lhs1[t, 0, :, p * N : (p + 1) * N] = high
            lhs1[t, 1, :, p * N : (p + 1) * N] = low
    for k, dy, dc in near:
        table_copy(k, dy, dc).wait()
    total = wall[0]
    for k in range(1, 8):
        total = total + wall[k]
    wsum[...] = total
    to_scalars = pltpu.make_async_copy(wsum, wsm, w_l)
    to_scalars.start()

    def set_rhs(top_real, top_imag, low_real, low_imag):
        for r, (left, right) in enumerate(((top_real, top_imag), (low_real, low_imag))):
            for q, value in enumerate((left, right)):
                high, low = halves(value)
                rhs[0, r * N : (r + 1) * N, q * N : (q + 1) * N] = high
                rhs[1, r * N : (r + 1) * N, q * N : (q + 1) * N] = low

    def dress(t):
        for dy in (1, 3, 2):
            tau_copy(t, dy).wait_recv()
            tau_forward(t, dy).start()
        tau_copy(t, 0).wait_recv()
        for dy in (1, 3, 2):
            tau_forward(t, dy).wait_recv()
        real, imag = taus[t, 0], taus[t, 1]
        set_rhs(real, imag, -imag, real)
        for p in range(2):
            high, low = halves(jnp.transpose(taus[t, p]))
            lhs2[0, :, p * N : (p + 1) * N] = high
            lhs2[1, :, p * N : (p + 1) * N] = low
        half = dot3(lhs1[t, 0], lhs1[t, 1], rhs[0], rhs[1])
        real, imag = half[:, :N], half[:, N:]
        set_rhs(real, imag, imag, -real)
        full = dot3(lhs2[0], lhs2[1], rhs[0], rhs[1])
        dres[t, 0] = full[:, :N]
        dres[t, 1] = full[:, N:]

    def turn(t):
        for p in range(2):
            for m in range(NCH):
                picked = jnp.concatenate(
                    [
                        dres[t, p, BLK * (2 * yy + cc) + SUB * m : BLK * (2 * yy + cc) + SUB * (m + 1), :]
                        for cc in range(2)
                        for yy in range(4)
                    ],
                    axis=0,
                )
                drest[t, p, :, CH * m : CH * (m + 1)] = jnp.transpose(picked)

    def b_copy(t, k, dy, dc):
        where = column(dy, dc, -1 if t == 0 else 0)
        return remote(
            dres.at[t, :, rows(where[0], BLK), :],
            bbuf.at[:, pl.ds(pl.multiple_of(t * N + op * BLK, 16), BLK), :],
            b_s.at[t, k], b_r.at[t, k], where,
        )

    def a_copy(t, m, k, dy, dc):
        where = column(dy, dc, 1 if t == 1 else 0)
        lanes = pl.ds(m * CH, CH)
        return remote(
            drest.at[t, :, rows(where[0], BLK), lanes],
            abuf.at[:, pl.ds(pl.multiple_of(t * N + op * BLK, 16), BLK), lanes],
            a_s.at[t, m, k], a_r.at[t, m, k], where,
        )

    def b_rels(t):
        return [(k, dy, dc) for k, (dy, dc) in enumerate(RELS) if t == 0 or (dy, dc) != (0, 0)]

    def a_rels(t):
        return [(k, dy, dc) for k, (dy, dc) in enumerate(RELS) if t == 1 or (dy, dc) != (0, 0)]

    dress(0)
    for k, dy, dc in b_rels(0):
        b_copy(0, k, dy, dc).start()
    turn(0)
    dress(1)
    for k, dy, dc in b_rels(1):
        b_copy(1, k, dy, dc).start()
    turn(1)
    for m in range(NCH):
        for t in range(2):
            for k, dy, dc in a_rels(t):
                a_copy(t, m, k, dy, dc).start()
    mine = rows(op, BLK)
    abuf[:, mine, :] = drest[0, :, mine, :]
    bbuf[:, pl.ds(pl.multiple_of(N + op * BLK, 16), BLK), :] = dres[1, :, mine, :]

    to_scalars.wait()

    def weigh(t):
        def body(n, carry):
            d, a = n // OPS, n % OPS
            for p in range(2):
                total = None
                for b in range(OPS):
                    weight = wsm[n // 16, (n % 16) * 8 + b]
                    term = weight * bbuf[p, t * N + b * BLK : t * N + (b + 1) * BLK, :]
                    total = term if total is None else total + term
                high, low = halves(total)
                where = pl.ds(pl.multiple_of(t * N + a * BLK, 16), BLK)
                ehi[d, where, p * N : (p + 1) * N] = high
                elo[d, where, p * N : (p + 1) * N] = low
            return carry

        lax.fori_loop(0, DIAG * OPS, body, 0)

    for t in range(2):
        for k, dy, dc in b_rels(t):
            b_copy(t, k, dy, dc).wait_recv()
        weigh(t)

    own = rows(c, HALF)
    other = rows(1 - c, HALF)

    def core_copy(m, d):
        zz, xx = d // 2, (d % 2) * 2
        return remote(
            prod.at[m, zz, pl.ds(xx, 2), other, :], cbuf.at[m, zz, pl.ds(xx, 2)],
            c_s.at[m, d], c_r.at[m, d], device(dc=1),
        )

    def main(m):
        for t in range(2):
            for k, dy, dc in a_rels(t):
                a_copy(t, m, k, dy, dc).wait_recv()
        for p in range(2):
            high, low = halves(jnp.transpose(abuf[p, :, m * CH : (m + 1) * CH]))
            lmain[0, p * CH : (p + 1) * CH, :] = high
            lmain[1, p * CH : (p + 1) * CH, :] = low

        def body(d, carry):
            both = dot3(lmain[0], lmain[1], ehi[d], elo[d])
            zz, xx = d // 2, (d % 2) * 2
            prod[m, zz, xx] = both[:CH, :N] - both[CH:, N:]
            prod[m, zz, xx + 1] = both[:CH, N:] + both[CH:, :N]
            core_copy(m, d).start()
            return carry

        lax.fori_loop(0, DIAG, body, 0)

    top = pl.ds(pl.multiple_of(c * HALF, HALF), HALF // 2)
    low_half = pl.ds(pl.multiple_of(c * HALF + HALF // 2, HALF // 2), HALF // 2)

    def x1_copy(m, k):
        return remote(
            prod.at[m, :, (x + k) % 4, top, :], s1x.at[m, k - 1], x1_s.at[m, k - 1], x1_r.at[m, k - 1], device(dx=k)
        )

    def z1_copy(m, k):
        return remote(
            prod.at[m, (z + k) % 4, :, low_half, :], s1z.at[m, k - 1], z1_s.at[m, k - 1], z1_r.at[m, k - 1], device(dz=k)
        )

    def z2_copy(m, k):
        return remote(r0.at[m, (z + k) % 4], s2z.at[m, k - 1], z2_s.at[m, k - 1], z2_r.at[m, k - 1], device(dz=k))

    def x2_copy(m, k):
        return remote(r1.at[m, (x + k) % 4], s2x.at[m, k - 1], x2_s.at[m, k - 1], x2_r.at[m, k - 1], device(dx=k))

    def y_copy(m, k):
        return remote(
            sbuf.at[m, rows((y + k) % 4, SUB), :], fin.at[m, k - 1], y_s.at[m, k - 1], y_r.at[m, k - 1], device(dy=k)
        )

    def stage0(m):
        def body(d, carry):
            core_copy(m, d).wait_recv()
            zz, xx = d // 2, (d % 2) * 2
            for p in range(2):
                prod[m, zz, xx + p, own, :] = prod[m, zz, xx + p, own, :] + cbuf[m, zz, xx + p]
            return carry

        lax.fori_loop(0, DIAG, body, 0)
        for k in (1, 3, 2):
            x1_copy(m, k).start()
            z1_copy(m, k).start()

    def stage1(m):
        for k in (1, 3, 2):
            x1_copy(m, k).wait_recv()
            z1_copy(m, k).wait_recv()
        for q in range(4):
            r0[m, q] = (prod[m, q, x, top, :] + s1x[m, 0, q]) + (s1x[m, 1, q] + s1x[m, 2, q])
            r1[m, q] = (prod[m, z, q, low_half, :] + s1z[m, 0, q]) + (s1z[m, 1, q] + s1z[m, 2, q])
        for k in (1, 3, 2):
            z2_copy(m, k).start()
            x2_copy(m, k).start()

    def stage2(m):
        for k in (1, 3, 2):
            z2_copy(m, k).wait_recv()
            x2_copy(m, k).wait_recv()
        sbuf[m, : HALF // 2] = (r0[m, z] + s2z[m, 0]) + (s2z[m, 1] + s2z[m, 2])
        sbuf[m, HALF // 2 :] = (r1[m, x] + s2x[m, 0]) + (s2x[m, 1] + s2x[m, 2])
        for k in (1, 3, 2):
            y_copy(m, k).start()

    def stage3(m):
        for k in (1, 3, 2):
            y_copy(m, k).wait_recv()
        out[m * SUB : (m + 1) * SUB, :] = (sbuf[m, rows(y, SUB), :] + fin[m, 0]) + (fin[m, 1] + fin[m, 2])

    main(0)
    stage0(0)
    main(1)
    stage0(1)
    stage1(0)
    main(2)
    stage0(2)
    stage1(1)
    stage2(0)
    stage1(2)
    stage2(1)
    stage3(0)
    stage2(2)
    stage3(1)
    stage3(2)

    for t in range(2):
        for dy in (1, 3, 2, 0):
            tau_copy(t, dy).wait_send()
        for dy in (1, 3, 2):
            tau_forward(t, dy).wait_send()
        for k, dy, dc in b_rels(t):
            b_copy(t, k, dy, dc).wait_send()
        for m in range(NCH):
            for k, dy, dc in a_rels(t):
                a_copy(t, m, k, dy, dc).wait_send()
    for m in range(NCH):
        for d in range(DIAG):
            core_copy(m, d).wait_send()
        for k in (1, 2, 3):
            for copy in (x1_copy, z1_copy, x2_copy, z2_copy, y_copy):
                copy(m, k).wait_send()


def local(mesons, perambulator, graph_list):
    times = mesons.shape[1] * lax.axis_size("tm")
    factor = (2.0 * N) ** (-0.5) / times
    place = (graph_list[:, 2] * OPS + graph_list[:, 0]) * OPS + graph_list[:, 1]
    weight = graph_list[:, 3].astype(F32) * factor
    table = jnp.sum(
        jnp.where(place[:, None, None] == jnp.arange(1024, dtype=jnp.int32).reshape(8, 128), weight[:, None, None], 0.0),
        axis=0,
    )
    dma = pltpu.SemaphoreType.DMA
    vmem = pltpu.VMEM
    q = HALF // 2
    return pl.pallas_call(
        kernel,
        out_shape=jax.ShapeDtypeStruct((BLK, N), F32),
        in_specs=[pl.BlockSpec(memory_space=pltpu.VMEM)] * 3,
        out_specs=pl.BlockSpec(memory_space=pltpu.VMEM),
        scratch_shapes=[
            vmem((8, 8, 128), F32), vmem((8, 128), F32), pltpu.SMEM((8, 128), F32),
            vmem((2, 2, N, N), F32),
            vmem((2, 2, N, 2 * N), BF16), vmem((2, N, 2 * N), BF16), vmem((2, 2 * N, 2 * N), BF16),
            vmem((2, 2, N, N), F32), vmem((2, 2, N, N), F32),
            vmem((2, 2 * N, N), F32), vmem((2, 2 * N, N), F32),
            vmem((DIAG, 2 * N, 2 * N), BF16), vmem((DIAG, 2 * N, 2 * N), BF16),
            vmem((2, 2 * CH, 2 * N), BF16),
            vmem((NCH, 4, 4, CH, N), F32), vmem((NCH, 4, 4, HALF, N), F32),
            vmem((NCH, 3, 4, q, N), F32), vmem((NCH, 3, 4, q, N), F32),
            vmem((NCH, 4, q, N), F32), vmem((NCH, 4, q, N), F32),
            vmem((NCH, 3, q, N), F32), vmem((NCH, 3, q, N), F32),
            vmem((NCH, HALF, N), F32), vmem((NCH, 3, SUB, N), F32),
            dma((8,)), dma((8,)), dma,
            dma((2, 4)), dma((2, 4)), dma((2, 4)), dma((2, 4)),
            dma((2, NCH, 8)), dma((2, NCH, 8)), dma((2, 8)), dma((2, 8)),
            dma((NCH, 8)), dma((NCH, 8)),
        ] + [dma((NCH, 3))] * 10,
        compiler_params=pltpu.CompilerParams(
            collective_id=0, has_side_effects=True, vmem_limit_bytes=64 * 2**20 - 2**19
        ),
    )(mesons, perambulator, table)


def solution(mesh):
    placed = (P("op", "tm", None, None, None), P("tm", None, "op", None), P("op", None))
    return jax.shard_map(
        local, mesh=mesh, in_specs=placed, out_specs=P("op", "tm"), check_vma=False
    )
```

```python
import functools

import jax
import jax.numpy as jnp
from jax import lax
from jax.experimental import pallas as pl
from jax.experimental.pallas import tpu as pltpu
from jax.sharding import PartitionSpec as P

N = 384
DIAG = 8
OPS = 8
BLK = N // 8
CH = 128
NCH = N // CH
HALF = CH // 2
SUB = HALF // 4
F32 = jnp.float32
BF16 = jnp.bfloat16
MESH = pl.DeviceIdType.MESH
RELS = [(dy, dc) for dy in (1, 3, 2, 0) for dc in (0, 1)]


def halves(value):
    high = value.astype(BF16)
    return high, (value - high.astype(F32)).astype(BF16)


def dot3(a_high, a_low, b_high, b_low):
    dot = functools.partial(jnp.dot, preferred_element_type=F32)
    return dot(a_high, b_high) + (dot(a_high, b_low) + dot(a_low, b_high))


def rows(index, size):
    return pl.ds(pl.multiple_of(index * size, size), size)


def kernel(
    mesons_hbm, tau, graph, out,
    mesons, table, wall, wide, kron, taus, lhs1, lhs2, rhs, dres, drest, abuf, bbuf, ehi, elo,
    prod, cbuf, s1, r1, s2, r2, s3,
    m_l, w_s, w_r, t_s, t_r, f_s, f_r, a_s, a_r, b_s, b_r, c_s, c_r,
    s1_s, s1_r, s2_s, s2_r, s3_s, s3_r,
):
    op, tm = lax.axis_index("op"), lax.axis_index("tm")
    y, c, z, x = op // 2, op % 2, tm // 4, tm % 4

    def device(dy=0, dc=0, dz=0, dx=0):
        return (((y + dy) % 4) * 2 + (c + dc) % 2, ((z + dz) % 4) * 4 + (x + dx) % 4)

    def column(dy, dc, dj):
        return (((y + dy) % 4) * 2 + (c + dc) % 2, (tm + dj + 16) % 16)

    def source(dy, dc):
        return ((y - dy + 4) % 4) * 2 + (c + dc) % 2

    def remote(src, dst, send, recv, where):
        return pltpu.make_async_remote_copy(
            src_ref=src, dst_ref=dst, send_sem=send, recv_sem=recv, device_id=where, device_id_type=MESH
        )

    sent = []

    def send(copy):
        copy.start()
        sent.append(copy)

    greet = [column(dy, dc, dj) for dj in (0, 1, -1) for dy, dc in RELS if (dy, dc, dj) != (0, 0, 0)]
    greet += [device(dx=k) for k in (1, 2, 3)] + [device(dz=k) for k in (1, 2, 3)]
    barrier = pltpu.get_barrier_semaphore()
    for where in greet:
        pl.semaphore_signal(barrier, inc=1, device_id=where, device_id_type=MESH)
    load = pltpu.make_async_copy(mesons_hbm.at[0], mesons, m_l)
    load.start()
    table[...] = jnp.zeros_like(table)
    table[:, 0:4] = graph[...]
    pl.semaphore_wait(barrier, len(greet))

    near = [(k, dy, dc) for k, (dy, dc) in enumerate(RELS) if (dy, dc) != (0, 0)]

    def tau_copy(t, dy):
        if dy == 2:
            via = 3 if t else 1
            block = taus.at[t, :, rows(source(via, 0), BLK), :]
            return remote(block, block, t_s.at[t, dy], t_r.at[t, dy], device(dy=via))
        dc = 1 if dy == 0 else 0
        return remote(
            tau.at[t], taus.at[t, :, rows(op, BLK), :], t_s.at[t, dy], t_r.at[t, dy], device(dy=dy, dc=dc)
        )

    def tau_forward(t, dy):
        block = taus.at[t, :, rows(source(dy, 0), BLK), :]
        return remote(block, block, f_s.at[t, dy], f_r.at[t, dy], device(dc=1))

    def table_copy(k, dy, dc):
        return remote(table, wall.at[op], w_s.at[k], w_r.at[k], device(dy=dy, dc=dc))

    for t, order in ((0, (1, 3, 0)), (1, (3, 1, 0))):
        for dy in order:
            send(tau_copy(t, dy))
    for k, dy, dc in near:
        send(table_copy(k, dy, dc))
    wall[op] = table[...]
    load.wait()
    for t in range(2):
        taus[t, :, rows(op, BLK), :] = tau[t]
        for p in range(2):
            high, low = halves(mesons[t, p])
            lhs1[t, 0, :, p * N : (p + 1) * N] = high
            lhs1[t, 1, :, p * N : (p + 1) * N] = low
    def set_rhs(top_real, top_imag, low_real, low_imag):
        for r, (left, right) in enumerate(((top_real, top_imag), (low_real, low_imag))):
            for q, value in enumerate((left, right)):
                high, low = halves(value)
                rhs[0, r * N : (r + 1) * N, q * N : (q + 1) * N] = high
                rhs[1, r * N : (r + 1) * N, q * N : (q + 1) * N] = low

    def pass_on(t, dy):
        tau_copy(t, dy).wait_recv()
        if dy == (3 if t else 1):
            send(tau_copy(t, 2))
        send(tau_forward(t, dy))

    def dress(t):
        tau_copy(t, 0).wait_recv()
        for dy in (1, 3, 2):
            tau_forward(t, dy).wait_recv()
        real, imag = taus[t, 0], taus[t, 1]
        set_rhs(real, imag, -imag, real)
        for p in range(2):
            high, low = halves(jnp.transpose(taus[t, p]))
            lhs2[0, :, p * N : (p + 1) * N] = high
            lhs2[1, :, p * N : (p + 1) * N] = low
        half = dot3(lhs1[t, 0], lhs1[t, 1], rhs[0], rhs[1])
        real, imag = half[:, :N], half[:, N:]
        set_rhs(real, imag, imag, -real)
        full = dot3(lhs2[0], lhs2[1], rhs[0], rhs[1])
        dres[t, 0] = full[:, :N]
        dres[t, 1] = full[:, N:]

    def turn(t):
        for p in range(2):
            for m in range(NCH):
                picked = jnp.concatenate(
                    [
                        dres[t, p, BLK * (2 * yy + cc) + SUB * m : BLK * (2 * yy + cc) + SUB * (m + 1), :]
                        for cc in range(2)
                        for yy in range(4)
                    ],
                    axis=0,
                )
                drest[t, p, :, CH * m : CH * (m + 1)] = jnp.transpose(picked)

    def b_copy(t, k, dy, dc):
        where = column(dy, dc, -1 if t == 0 else 0)
        return remote(
            dres.at[t, :, rows(where[0], BLK), :],
            bbuf.at[:, pl.ds(pl.multiple_of(t * N + op * BLK, 16), BLK), :],
            b_s.at[t, k], b_r.at[t, k], where,
        )

    def a_copy(t, m, k, dy, dc):
        where = column(dy, dc, 1 if t == 1 else 0)
        lanes = pl.ds(m * CH, CH)
        return remote(
            drest.at[t, :, rows(where[0], BLK), lanes],
            abuf.at[:, pl.ds(pl.multiple_of(t * N + op * BLK, 16), BLK), lanes],
            a_s.at[t, m, k], a_r.at[t, m, k], where,
        )

    def b_rels(t):
        return [(k, dy, dc) for k, (dy, dc) in enumerate(RELS) if t == 0 or (dy, dc) != (0, 0)]

    def a_rels(t):
        return [(k, dy, dc) for k, (dy, dc) in enumerate(RELS) if t == 1 or (dy, dc) != (0, 0)]

    def send_a(m):
        for t in range(2):
            for k, dy, dc in a_rels(t):
                send(a_copy(t, m, k, dy, dc))

    for t, dy in ((0, 1), (0, 3), (1, 3), (0, 2)):
        pass_on(t, dy)
    dress(0)
    for dy in (1, 2):
        pass_on(1, dy)
    for k, dy, dc in b_rels(0):
        send(b_copy(0, k, dy, dc))
    dress(1)
    for k, dy, dc in b_rels(1):
        send(b_copy(1, k, dy, dc))
    turn(0)
    turn(1)
    send_a(0)
    mine = rows(op, BLK)
    abuf[:, mine, :] = drest[0, :, mine, :]
    bbuf[:, pl.ds(pl.multiple_of(N + op * BLK, 16), BLK), :] = dres[1, :, mine, :]
    for k, dy, dc in near:
        table_copy(k, dy, dc).wait_recv()
    slots = wall[...].reshape(64, 128)
    left = lax.broadcasted_iota(jnp.int32, (64, 128), 1) == slots[:, 2:3] * OPS + slots[:, 0:1]
    left = jnp.transpose(jnp.where(left, slots[:, 3:4].astype(F32), 0.0))
    right = lax.broadcasted_iota(jnp.int32, (64, N), 1) // BLK == slots[:, 1:2]
    wide[...] = jnp.dot(
        left[: DIAG * OPS].astype(BF16), right.astype(F32).astype(BF16), preferred_element_type=F32
    )
    same = lax.broadcasted_iota(jnp.int32, (BLK, N), 0) == lax.broadcasted_iota(jnp.int32, (BLK, N), 1) % BLK

    def widen(d, carry):
        for a in range(OPS):
            block = jnp.where(same, wide[pl.ds(d * OPS + a, 1), :], 0.0).astype(BF16)
            kron[d, a * BLK : (a + 1) * BLK, :N] = block
            kron[d, a * BLK : (a + 1) * BLK, N:] = block
        return carry

    lax.fori_loop(0, DIAG, widen, 0)

    xcat, lmain = rhs.at[0], lhs2.at[:, : 2 * CH, :]

    def weigh(t):
        for p in range(2):
            high, low = halves(bbuf[p, t * N : (t + 1) * N, :])
            xcat[:N, p * N : (p + 1) * N] = high
            xcat[N:, p * N : (p + 1) * N] = low

        def body(d, carry):
            high, low = halves(jnp.dot(kron[d], xcat[...], preferred_element_type=F32))
            ehi[d, t * N : (t + 1) * N, :] = high
            elo[d, t * N : (t + 1) * N, :] = low
            return carry

        lax.fori_loop(0, DIAG, body, 0)

    for t in range(2):
        for k, dy, dc in b_rels(t):
            b_copy(t, k, dy, dc).wait_recv()
        weigh(t)
        send_a(t + 1)

    own, other = pl.ds(c * 4, 4), pl.ds((1 - c) * 4, 4)

    def core_copy(m, d):
        zz, xx = d // 2, (d % 2) * 2
        return remote(
            prod.at[m, zz, pl.ds(xx, 2), other], cbuf.at[m, zz, pl.ds(xx, 2)],
            c_s.at[m, d], c_r.at[m, d], device(dc=1),
        )

    def main(m):
        for t in range(2):
            for k, dy, dc in a_rels(t):
                a_copy(t, m, k, dy, dc).wait_recv()
        for p in range(2):
            high, low = halves(jnp.transpose(abuf[p, :, m * CH : (m + 1) * CH]))
            lmain[0, p * CH : (p + 1) * CH, :] = high
            lmain[1, p * CH : (p + 1) * CH, :] = low

        def body(d, carry):
            both = dot3(lmain[0], lmain[1], ehi[d], elo[d])
            zz, xx = d // 2, (d % 2) * 2
            prod[m, zz, xx] = (both[:CH, :N] - both[CH:, N:]).reshape(8, SUB, N)
            prod[m, zz, xx + 1] = (both[:CH, N:] + both[CH:, :N]).reshape(8, SUB, N)
            core_copy(m, d).start()
            return carry

        lax.fori_loop(0, DIAG, body, 0)

    def hop(axis, k):
        return device(**{"d" + axis: k})

    def first_part(m, p, k):
        lanes = pl.ds(CH * p, CH)
        if p == 0:
            return prod.at[m, :, (x + k) % 4, own, :, lanes]
        if p == 1:
            return prod.at[m, (z + k) % 4, :, own, :, lanes]
        return prod.at[m, :, :, c * 4 + (y + k) % 4, :, lanes]

    def second_part(m, p, k):
        if p == 0:
            return r1.at[m, p, (z + k) % 4]
        return r1.at[m, p, :, ((y if p == 1 else x) + k) % 4]

    def third_part(m, p, k):
        return r2.at[m, p, ((y, x, z)[p] + k) % 4]

    def first_copy(m, p, k):
        return remote(
            first_part(m, p, k), s1.at[m, p, k - 1], s1_s.at[m, p, k - 1], s1_r.at[m, p, k - 1], hop("xzy"[p], k)
        )

    def second_copy(m, p, k):
        return remote(
            second_part(m, p, k), s2.at[m, p, k - 1], s2_s.at[m, p, k - 1], s2_r.at[m, p, k - 1], hop("zyx"[p], k)
        )

    def third_copy(m, p, k):
        return remote(
            third_part(m, p, k), s3.at[m, p, k - 1], s3_s.at[m, p, k - 1], s3_r.at[m, p, k - 1], hop("yxz"[p], k)
        )

    def start_all(copy, m):
        for k in (1, 3, 2):
            for p in range(3):
                send(copy(m, p, k))

    def stage0(m):
        def body(d, carry):
            core_copy(m, d).wait_recv()
            zz, xx = d // 2, (d % 2) * 2
            for p in range(2):
                prod[m, zz, xx + p, own] = prod[m, zz, xx + p, own] + cbuf[m, zz, xx + p]
            return carry

        lax.fori_loop(0, DIAG, body, 0)
        start_all(first_copy, m)

    def stage1(m):
        for p in range(3):
            for k in (1, 3, 2):
                first_copy(m, p, k).wait_recv()
            r1[m, p] = (first_part(m, p, 0)[...] + s1[m, p, 0]) + (s1[m, p, 1] + s1[m, p, 2])
            for k in (1, 3, 2):
                send(second_copy(m, p, k))

    def stage2(m):
        for p in range(3):
            for k in (1, 3, 2):
                second_copy(m, p, k).wait_recv()
            r2[m, p] = (second_part(m, p, 0)[...] + s2[m, p, 0]) + (s2[m, p, 1] + s2[m, p, 2])
            for k in (1, 3, 2):
                send(third_copy(m, p, k))

    def stage3(m):
        for p in range(3):
            for k in (1, 3, 2):
                third_copy(m, p, k).wait_recv()
            total = (third_part(m, p, 0)[...] + s3[m, p, 0]) + (s3[m, p, 1] + s3[m, p, 2])
            total = total * ((2.0 * N) ** (-0.5) / (2 * lax.axis_size("tm")))
            out[m * SUB : (m + 1) * SUB, p * CH : (p + 1) * CH] = total

    main(0)
    stage0(0)
    main(1)
    stage0(1)
    stage1(0)
    main(2)
    stage0(2)
    stage1(1)
    stage2(0)
    stage1(2)
    stage2(1)
    stage3(0)
    stage2(2)
    stage3(1)
    stage3(2)

    for copy in sent:
        copy.wait_send()
    for m in range(NCH):
        for d in range(DIAG):
            core_copy(m, d).wait_send()


def local(mesons, perambulator, graph_list):
    dma = pltpu.SemaphoreType.DMA
    vmem = pltpu.VMEM
    return pl.pallas_call(
        kernel,
        out_shape=jax.ShapeDtypeStruct((BLK, N), F32),
        in_specs=[pl.BlockSpec(memory_space=pl.ANY)] + [pl.BlockSpec(memory_space=pltpu.VMEM)] * 2,
        out_specs=pl.BlockSpec(memory_space=pltpu.VMEM),
        scratch_shapes=[
            vmem((2, 2, N, N), F32), vmem((8, 128), jnp.int32),
            vmem((8, 8, 128), jnp.int32), vmem((DIAG * OPS, N), F32), vmem((DIAG, N, 2 * N), BF16),
            vmem((2, 2, N, N), F32),
            vmem((2, 2, N, 2 * N), BF16), vmem((2, N, 2 * N), BF16), vmem((2, 2 * N, 2 * N), BF16),
            vmem((2, 2, N, N), F32), vmem((2, 2, N, N), F32),
            vmem((2, 2 * N, N), F32), vmem((2, 2 * N, N), F32),
            vmem((DIAG, 2 * N, 2 * N), BF16), vmem((DIAG, 2 * N, 2 * N), BF16),
            vmem((NCH, 4, 4, 8, SUB, N), F32), vmem((NCH, 4, 4, 4, SUB, N), F32),
            vmem((NCH, 3, 3, 4, 4, SUB, CH), F32), vmem((NCH, 3, 4, 4, SUB, CH), F32),
            vmem((NCH, 3, 3, 4, SUB, CH), F32), vmem((NCH, 3, 4, SUB, CH), F32), vmem((NCH, 3, 3, SUB, CH), F32),
            dma, dma((8,)), dma((8,)),
            dma((2, 4)), dma((2, 4)), dma((2, 4)), dma((2, 4)),
            dma((2, NCH, 8)), dma((2, NCH, 8)), dma((2, 8)), dma((2, 8)),
            dma((NCH, 8)), dma((NCH, 8)),
        ] + [dma((NCH, 3, 3))] * 6,
        compiler_params=pltpu.CompilerParams(
            collective_id=0, has_side_effects=True, vmem_limit_bytes=64 * 2**20 - 2**19
        ),
    )(mesons, perambulator, graph_list)


def solution(mesh):
    placed = (P("op", "tm", None, None, None), P("tm", None, "op", None), P("op", None))
    return jax.shard_map(
        local, mesh=mesh, in_specs=placed, out_specs=P("op", "tm"), check_vma=False
    )
```

```python
import functools

import jax
import jax.numpy as jnp
from jax import lax
from jax.experimental import pallas as pl
from jax.experimental.pallas import tpu as pltpu
from jax.sharding import PartitionSpec as P

N = 384
DIAG = 8
OPS = 8
BLK = N // 8
CH = 128
NCH = N // CH
HALF = CH // 2
SUB = HALF // 4
F32 = jnp.float32
BF16 = jnp.bfloat16
MESH = pl.DeviceIdType.MESH
RELS = [(1, 0), (3, 0), (2, 0), (0, 1), (3, 1), (1, 1), (2, 1), (0, 0)]


def halves(value):
    high = value.astype(BF16)
    return high, (value - high.astype(F32)).astype(BF16)


def dot3(a_high, a_low, b_high, b_low):
    dot = functools.partial(jnp.dot, preferred_element_type=F32)
    return dot(a_high, b_high) + (dot(a_high, b_low) + dot(a_low, b_high))


def rows(index, size):
    return pl.ds(pl.multiple_of(index * size, size), size)


def kernel(
    mesons_hbm, tau, graph, out,
    mesons, table, wall, wide, kron, taus, lhs1, lhs2, rhs, dres, drest, abuf, bbuf, ehi, elo,
    prod, cbuf, s1, r1, s2, r2, s3,
    m_l, w_s, w_r, t_s, t_r, f_s, f_r, a_s, a_r, b_s, b_r, c_s, c_r,
    s1_s, s1_r, s2_s, s2_r, s3_s, s3_r,
):
    op, tm = lax.axis_index("op"), lax.axis_index("tm")
    y, c, z, x = op // 2, op % 2, tm // 4, tm % 4

    def device(dy=0, dc=0, dz=0, dx=0):
        return (((y + dy) % 4) * 2 + (c + dc) % 2, ((z + dz) % 4) * 4 + (x + dx) % 4)

    def column(dy, dc, dj):
        return (((y + dy) % 4) * 2 + (c + dc) % 2, (tm + dj + 16) % 16)

    def source(dy, dc):
        return ((y - dy + 4) % 4) * 2 + (c + dc) % 2

    def remote(src, dst, send, recv, where):
        return pltpu.make_async_remote_copy(
            src_ref=src, dst_ref=dst, send_sem=send, recv_sem=recv, device_id=where, device_id_type=MESH
        )

    sent = []

    def send(copy):
        copy.start()
        sent.append(copy)

    greet = [column(dy, dc, dj) for dj in (0, 1, -1) for dy, dc in RELS if (dy, dc, dj) != (0, 0, 0)]
    greet += [device(dx=k) for k in (1, 2, 3)] + [device(dz=k) for k in (1, 2, 3)]
    barrier = pltpu.get_barrier_semaphore()
    for where in greet:
        pl.semaphore_signal(barrier, inc=1, device_id=where, device_id_type=MESH)
    load = pltpu.make_async_copy(mesons_hbm.at[0], mesons, m_l)
    load.start()
    table[...] = jnp.zeros_like(table)
    table[:, 0:4] = graph[...]
    pl.semaphore_wait(barrier, len(greet))

    near = [(k, dy, dc) for k, (dy, dc) in enumerate(RELS) if (dy, dc) != (0, 0)]

    def tau_copy(t, dy):
        if dy == 2:
            via = 3 if t else 1
            block = taus.at[t, :, rows(source(via, 0), BLK), :]
            return remote(block, block, t_s.at[t, dy], t_r.at[t, dy], device(dy=via))
        dc = 1 if dy == 0 else 0
        return remote(
            tau.at[t], taus.at[t, :, rows(op, BLK), :], t_s.at[t, dy], t_r.at[t, dy], device(dy=dy, dc=dc)
        )

    def tau_forward(t, dy):
        block = taus.at[t, :, rows(source(dy, 0), BLK), :]
        return remote(block, block, f_s.at[t, dy], f_r.at[t, dy], device(dc=1))

    def table_copy(k, dy, dc):
        return remote(table, wall.at[op], w_s.at[k], w_r.at[k], device(dy=dy, dc=dc))

    for t, order in ((0, (1, 3, 0)), (1, (3, 1, 0))):
        for dy in order:
            send(tau_copy(t, dy))
    for k, dy, dc in near:
        send(table_copy(k, dy, dc))
    wall[op] = table[...]
    load.wait()
    for t in range(2):
        taus[t, :, rows(op, BLK), :] = tau[t]
        for p in range(2):
            high, low = halves(mesons[t, p])
            lhs1[t, 0, :, p * N : (p + 1) * N] = high
            lhs1[t, 1, :, p * N : (p + 1) * N] = low
    def set_rhs(top_real, top_imag, low_real, low_imag):
        for r, (left, right) in enumerate(((top_real, top_imag), (low_real, low_imag))):
            for q, value in enumerate((left, right)):
                high, low = halves(value)
                rhs[0, r * N : (r + 1) * N, q * N : (q + 1) * N] = high
                rhs[1, r * N : (r + 1) * N, q * N : (q + 1) * N] = low

    def pass_on(t, dy):
        tau_copy(t, dy).wait_recv()
        if dy == (3 if t else 1):
            send(tau_copy(t, 2))
        send(tau_forward(t, dy))

    def dress(t):
        tau_copy(t, 0).wait_recv()
        for dy in (1, 3, 2):
            tau_forward(t, dy).wait_recv()
        real, imag = taus[t, 0], taus[t, 1]
        set_rhs(real, imag, -imag, real)
        for p in range(2):
            high, low = halves(jnp.transpose(taus[t, p]))
            lhs2[0, :, p * N : (p + 1) * N] = high
            lhs2[1, :, p * N : (p + 1) * N] = low
        half = dot3(lhs1[t, 0], lhs1[t, 1], rhs[0], rhs[1])
        real, imag = half[:, :N], half[:, N:]
        set_rhs(real, imag, imag, -real)
        full = dot3(lhs2[0], lhs2[1], rhs[0], rhs[1])
        dres[t, 0] = full[:, :N]
        dres[t, 1] = full[:, N:]

    def turn(t):
        for p in range(2):
            for m in range(NCH):
                picked = jnp.concatenate(
                    [
                        dres[t, p, BLK * (2 * yy + cc) + SUB * m : BLK * (2 * yy + cc) + SUB * (m + 1), :]
                        for cc in range(2)
                        for yy in range(4)
                    ],
                    axis=0,
                )
                drest[t, p, :, CH * m : CH * (m + 1)] = jnp.transpose(picked)

    def b_copy(t, k, dy, dc):
        where = column(dy, dc, -1 if t == 0 else 0)
        return remote(
            dres.at[t, :, rows(where[0], BLK), :],
            bbuf.at[:, pl.ds(pl.multiple_of(t * N + op * BLK, 16), BLK), :],
            b_s.at[t, k], b_r.at[t, k], where,
        )

    def a_copy(t, m, k, dy, dc):
        where = column(dy, dc, 1 if t == 1 else 0)
        lanes = pl.ds(m * CH, CH)
        return remote(
            drest.at[t, :, rows(where[0], BLK), lanes],
            abuf.at[:, pl.ds(pl.multiple_of(t * N + op * BLK, 16), BLK), lanes],
            a_s.at[t, m, k], a_r.at[t, m, k], where,
        )

    def b_rels(t):
        return [(k, dy, dc) for k, (dy, dc) in enumerate(RELS) if t == 0 or (dy, dc) != (0, 0)]

    def a_rels(t):
        return [(k, dy, dc) for k, (dy, dc) in enumerate(RELS) if t == 1 or (dy, dc) != (0, 0)]

    def send_a(m):
        for t in range(2):
            for k, dy, dc in a_rels(t):
                send(a_copy(t, m, k, dy, dc))

    for t, dy in ((0, 1), (0, 3), (1, 3), (0, 2)):
        pass_on(t, dy)
    dress(0)
    for dy in (1, 2):
        pass_on(1, dy)
    for k, dy, dc in b_rels(0):
        send(b_copy(0, k, dy, dc))
    dress(1)
    for k, dy, dc in b_rels(1):
        send(b_copy(1, k, dy, dc))
    turn(0)
    turn(1)
    send_a(0)
    mine = rows(op, BLK)
    abuf[:, mine, :] = drest[0, :, mine, :]
    bbuf[:, pl.ds(pl.multiple_of(N + op * BLK, 16), BLK), :] = dres[1, :, mine, :]
    for k, dy, dc in near:
        table_copy(k, dy, dc).wait_recv()
    slots = wall[...].reshape(64, 128)
    left = lax.broadcasted_iota(jnp.int32, (64, 128), 1) == slots[:, 2:3] * OPS + slots[:, 0:1]
    left = jnp.transpose(jnp.where(left, slots[:, 3:4].astype(F32), 0.0))
    right = lax.broadcasted_iota(jnp.int32, (64, N), 1) // BLK == slots[:, 1:2]
    wide[...] = jnp.dot(
        left[: DIAG * OPS].astype(BF16), right.astype(F32).astype(BF16), preferred_element_type=F32
    )
    same = lax.broadcasted_iota(jnp.int32, (BLK, N), 0) == lax.broadcasted_iota(jnp.int32, (BLK, N), 1) % BLK

    def widen(d, carry):
        for a in range(OPS):
            block = jnp.where(same, wide[pl.ds(d * OPS + a, 1), :], 0.0).astype(BF16)
            kron[d, a * BLK : (a + 1) * BLK, :N] = block
            kron[d, a * BLK : (a + 1) * BLK, N:] = block
        return carry

    lax.fori_loop(0, DIAG, widen, 0)

    xcat, lmain = rhs.at[0], lhs2.at[:, : 2 * CH, :]

    def weigh(t):
        for p in range(2):
            high, low = halves(bbuf[p, t * N : (t + 1) * N, :])
            xcat[:N, p * N : (p + 1) * N] = high
            xcat[N:, p * N : (p + 1) * N] = low

        def body(d, carry):
            high, low = halves(jnp.dot(kron[d], xcat[...], preferred_element_type=F32))
            ehi[d, t * N : (t + 1) * N, :] = high
            elo[d, t * N : (t + 1) * N, :] = low
            return carry

        lax.fori_loop(0, DIAG, body, 0)

    for t in range(2):
        for k, dy, dc in b_rels(t):
            b_copy(t, k, dy, dc).wait_recv()
        weigh(t)
        send_a(t + 1)

    own, other = pl.ds(c * 4, 4), pl.ds((1 - c) * 4, 4)

    def core_copy(m, d):
        zz, xx = d // 2, (d % 2) * 2
        return remote(
            prod.at[m, zz, pl.ds(xx, 2), other], cbuf.at[m, zz, pl.ds(xx, 2)],
            c_s.at[m, d], c_r.at[m, d], device(dc=1),
        )

    def main(m):
        for t in range(2):
            for k, dy, dc in a_rels(t):
                a_copy(t, m, k, dy, dc).wait_recv()
        for p in range(2):
            high, low = halves(jnp.transpose(abuf[p, :, m * CH : (m + 1) * CH]))
            lmain[0, p * CH : (p + 1) * CH, :] = high
            lmain[1, p * CH : (p + 1) * CH, :] = low

        def body(d, carry):
            both = dot3(lmain[0], lmain[1], ehi[d], elo[d])
            zz, xx = d // 2, (d % 2) * 2
            prod[m, zz, xx] = (both[:CH, :N] - both[CH:, N:]).reshape(8, SUB, N)
            prod[m, zz, xx + 1] = (both[:CH, N:] + both[CH:, :N]).reshape(8, SUB, N)
            core_copy(m, d).start()
            return carry

        lax.fori_loop(0, DIAG, body, 0)

    def hop(axis, k):
        return device(**{"d" + axis: k})

    def first_part(m, p, k):
        lanes = pl.ds(CH * p, CH)
        if p == 0:
            return prod.at[m, :, (x + k) % 4, own, :, lanes]
        if p == 1:
            return prod.at[m, (z + k) % 4, :, own, :, lanes]
        return prod.at[m, :, :, c * 4 + (y + k) % 4, :, lanes]

    def second_part(m, p, k):
        if p == 0:
            return r1.at[m, p, (z + k) % 4]
        return r1.at[m, p, :, ((y if p == 1 else x) + k) % 4]

    def third_part(m, p, k):
        return r2.at[m, p, ((y, x, z)[p] + k) % 4]

    def first_copy(m, p, k):
        return remote(
            first_part(m, p, k), s1.at[m, p, k - 1], s1_s.at[m, p, k - 1], s1_r.at[m, p, k - 1], hop("xzy"[p], k)
        )

    def second_copy(m, p, k):
        return remote(
            second_part(m, p, k), s2.at[m, p, k - 1], s2_s.at[m, p, k - 1], s2_r.at[m, p, k - 1], hop("zyx"[p], k)
        )

    def third_copy(m, p, k):
        return remote(
            third_part(m, p, k), s3.at[m, p, k - 1], s3_s.at[m, p, k - 1], s3_r.at[m, p, k - 1], hop("yxz"[p], k)
        )

    def start_all(copy, m):
        for k in (1, 3, 2):
            for p in range(3):
                send(copy(m, p, k))

    def stage0(m):
        def body(d, carry):
            core_copy(m, d).wait_recv()
            zz, xx = d // 2, (d % 2) * 2
            for p in range(2):
                prod[m, zz, xx + p, own] = prod[m, zz, xx + p, own] + cbuf[m, zz, xx + p]
            return carry

        lax.fori_loop(0, DIAG, body, 0)
        start_all(first_copy, m)

    def stage1(m):
        for p in range(3):
            for k in (1, 3, 2):
                first_copy(m, p, k).wait_recv()
            r1[m, p] = (first_part(m, p, 0)[...] + s1[m, p, 0]) + (s1[m, p, 1] + s1[m, p, 2])
            for k in (1, 3, 2):
                send(second_copy(m, p, k))

    def stage2(m):
        for p in range(3):
            for k in (1, 3, 2):
                second_copy(m, p, k).wait_recv()
            r2[m, p] = (second_part(m, p, 0)[...] + s2[m, p, 0]) + (s2[m, p, 1] + s2[m, p, 2])
            for k in (1, 3, 2):
                send(third_copy(m, p, k))

    def stage3(m):
        for p in range(3):
            for k in (1, 3, 2):
                third_copy(m, p, k).wait_recv()
            total = (third_part(m, p, 0)[...] + s3[m, p, 0]) + (s3[m, p, 1] + s3[m, p, 2])
            total = total * ((2.0 * N) ** (-0.5) / (2 * lax.axis_size("tm")))
            out[m * SUB : (m + 1) * SUB, p * CH : (p + 1) * CH] = total

    main(0)
    stage0(0)
    main(1)
    stage0(1)
    stage1(0)
    main(2)
    stage0(2)
    stage1(1)
    stage2(0)
    stage1(2)
    stage2(1)
    stage3(0)
    stage2(2)
    stage3(1)
    stage3(2)

    for copy in sent:
        copy.wait_send()
    for m in range(NCH):
        for d in range(DIAG):
            core_copy(m, d).wait_send()


def local(mesons, perambulator, graph_list):
    dma = pltpu.SemaphoreType.DMA
    vmem = pltpu.VMEM
    return pl.pallas_call(
        kernel,
        out_shape=jax.ShapeDtypeStruct((BLK, N), F32),
        in_specs=[pl.BlockSpec(memory_space=pl.ANY)] + [pl.BlockSpec(memory_space=pltpu.VMEM)] * 2,
        out_specs=pl.BlockSpec(memory_space=pltpu.VMEM),
        scratch_shapes=[
            vmem((2, 2, N, N), F32), vmem((8, 128), jnp.int32),
            vmem((8, 8, 128), jnp.int32), vmem((DIAG * OPS, N), F32), vmem((DIAG, N, 2 * N), BF16),
            vmem((2, 2, N, N), F32),
            vmem((2, 2, N, 2 * N), BF16), vmem((2, N, 2 * N), BF16), vmem((2, 2 * N, 2 * N), BF16),
            vmem((2, 2, N, N), F32), vmem((2, 2, N, N), F32),
            vmem((2, 2 * N, N), F32), vmem((2, 2 * N, N), F32),
            vmem((DIAG, 2 * N, 2 * N), BF16), vmem((DIAG, 2 * N, 2 * N), BF16),
            vmem((NCH, 4, 4, 8, SUB, N), F32), vmem((NCH, 4, 4, 4, SUB, N), F32),
            vmem((NCH, 3, 3, 4, 4, SUB, CH), F32), vmem((NCH, 3, 4, 4, SUB, CH), F32),
            vmem((NCH, 3, 3, 4, SUB, CH), F32), vmem((NCH, 3, 4, SUB, CH), F32), vmem((NCH, 3, 3, SUB, CH), F32),
            dma, dma((8,)), dma((8,)),
            dma((2, 4)), dma((2, 4)), dma((2, 4)), dma((2, 4)),
            dma((2, NCH, 8)), dma((2, NCH, 8)), dma((2, 8)), dma((2, 8)),
            dma((NCH, 8)), dma((NCH, 8)),
        ] + [dma((NCH, 3, 3))] * 6,
        compiler_params=pltpu.CompilerParams(
            collective_id=0, has_side_effects=True, vmem_limit_bytes=64 * 2**20 - 2**19
        ),
    )(mesons, perambulator, graph_list)


def solution(mesh):
    placed = (P("op", "tm", None, None, None), P("tm", None, "op", None), P("op", None))
    return jax.shard_map(
        local, mesh=mesh, in_specs=placed, out_specs=P("op", "tm"), check_vma=False
    )
```
